32 devices in a mesh: rep: 2 (over y), exp: 8 (over z, core), ffn: 2 (over x).
Axes of the slice: x: 2, y: 2, z: 4, core: 2. Of those that a mesh axis runs over, the one named last changes fastest.
Arguments:
- out_grad: bfloat16 [128, 6144], P(('rep', 'exp', 'ffn')), may hold values from -6 to 6
- experts: int32 [128, 4], P(('rep', 'exp', 'ffn')), may hold values from 0 to 7, all different within a row; in each aligned block of 4 rows (0 to 3, 4 to 7, ...) at most 4 rows name the same one
- gates: float32 [128, 4], P(('rep', 'exp', 'ffn')), may hold values from 0.1 to 1
- expert_inputs: bfloat16 [2, 8, 64, 6144], P('rep', 'exp'), may hold values from -6 to 6
- w_in: bfloat16 [8, 6144, 256], P('exp', None, 'ffn'), may hold values from -0.078125 to 0.078125
- w_lin: bfloat16 [8, 6144, 256], P('exp', None, 'ffn'), may hold values from -0.078125 to 0.078125
- w_out: bfloat16 [8, 256, 6144], P('exp', 'ffn'), may hold values from -0.375 to 0.375
Outputs:
- grad_input: bfloat16 [128, 6144], P(('rep', 'exp', 'ffn'))
- grad_w1: float32 [8, 6144, 256], P('exp', 'rep', 'ffn')
- grad_v1: float32 [8, 6144, 256], P('exp', 'rep', 'ffn')
- grad_w2: float32 [8, 256, 6144], P('exp', 'ffn', 'rep')
The draws below stay inside these ranges and needn't reach their ends.
Inputs may be any that keep to these rules, and one draw needn't show every extreme that they name: Each token names 4 different experts; the tokens of one device name one expert at most 4 times, and in every draw some device names some expert exactly 4 times.
All inputs are finite; a program needn't handle non-finite values.
Results may differ from the reference program's by a relative error of at most 0.0073.
Values may be sent and summed in bfloat16 or wider, within the bound.
No kernel may reach another device: no remote copies, remote signals or barrier semaphores. Data moves between devices by JAX's collectives and lax.ppermute only.
A program may use at most 64 MiB of HBM per device.

```python
import math
import jax
import jax.numpy as jnp
import numpy as np
from jax import lax

D = 6144
EXPERTS = 8
TOP = 4
FF_DEV = 128
FF = 256
TOK_DEV = 4
CAP = 4
ROWS = 64
TOKENS = 128
N_REP = 2
N_EXP = 8
N_FFN = 2


def levels(rng, shape, shards, least, largest):
    def one(dim, shards_of):
        steps = jax.random.uniform(jax.random.fold_in(jax.random.fold_in(rng, 6), dim), (shards_of,), jnp.float32, least / len(shards), largest / len(shards))
        return jnp.repeat(jnp.exp(steps), shape[dim] // shards_of).reshape((-1,) + (1,) * (len(shape) - dim - 1))

    loudness = one(*shards[0])
    for cut in shards[1:]:
        loudness = loudness * one(*cut)
    return loudness


def assign_block(rng, own, number, rows, number_of, top, most, skew):
    order = jax.random.permutation(rng, number_of)
    heavy_load, ordinary = load_shares(number_of, rows * top, most, skew, True), load_shares(number_of, rows * top, most, skew, False)
    places = jnp.arange(number_of)

    def named(sizes, turn):
        used = int((sizes > 0).sum())
        fixed = max(1, used // 4)
        shifted = fixed + (places - fixed + turn * (used - fixed)) % max(1, number_of - fixed)
        return jnp.zeros((number_of,), jnp.int32).at[order[jnp.where(places < fixed, places, shifted)]].set(jnp.asarray(sizes, jnp.int32))

    sizes = jnp.where(number % 4 == 0, named(heavy_load, number // 4), named(ordinary, number - number // 4 - 1))
    mixed = jax.random.permutation(jax.random.fold_in(own, 3), number_of)
    source_of, sink = mixed[0:number_of // 2 * 2:2], mixed[1:number_of // 2 * 2:2]
    room = jnp.minimum(sizes[source_of] - 1, most - sizes[sink]) // 2
    room = jnp.where((source_of == order[0]) | (sink == order[0]) | (sizes[sink] == 0), 0, jnp.maximum(room, 0))
    shifted = jax.random.randint(jax.random.fold_in(own, 4), (number_of // 2,), 0, 1 << 20) % (room + 1)
    sizes = sizes.at[source_of].add(-shifted).at[sink].add(shifted)
    members = jnp.searchsorted(jnp.cumsum(sizes), jnp.arange(rows * top), side="right").astype(jnp.int32)
    listing = members.reshape(top, rows).T
    listing = listing[jax.random.permutation(jax.random.fold_in(own, 1), rows)]
    turn = jax.random.randint(jax.random.fold_in(own, 2), (rows, 1), 0, top)
    return jnp.take_along_axis(listing, (jnp.arange(top)[None, :] + turn) % top, axis=1)


def load_shares(amount, total, most, lean, full):
    loads = [(1 << 20) // math.isqrt(standing ** lean) + 1 for standing in range(1, amount + 1)]
    largest = most if full else min(most, max(-(-total // amount), total * loads[0] // sum(loads)))
    least = 1 if total - largest >= amount - 1 else 0
    counts, rest = [largest] + [least] * (amount - 1), total - largest - least * (amount - 1)
    while rest > 0:
        movable = [i for i in range(1, amount) if counts[i] < largest] or [i for i in range(1, amount) if counts[i] < most]
        mass, remaining = sum([loads[i] for i in movable]), rest
        for i in movable:
            more = min(most - counts[i], max(1, remaining * loads[i] // mass), rest)
            counts[i] = counts[i] + more
            rest = rest - more
    return np.array(counts)


def bell_draw(rng, extent, width, limit, pieces=(), held_as=jnp.bfloat16):
    entries = jax.random.normal(rng, extent, jnp.float32) * width
    if len(pieces) > 0:
        entries = levels(rng, extent, pieces, -0.22, 0.18) * entries
    return jnp.clip(entries, min=-limit, max=limit).astype(held_as)


def setup_inputs(seed: int = 0) -> dict:
    arg_keys = jax.random.split(jax.random.key(seed), 8)
    out_grad = bell_draw(arg_keys[0], (TOKENS, D), 1.0, 6.0, ((0, 32),))
    experts_keys = jax.random.split(jax.random.fold_in(arg_keys[1], 1), TOKENS // TOK_DEV)
    experts_turns = jax.random.permutation(jax.random.fold_in(arg_keys[1], 3), TOKENS // TOK_DEV)
    experts = jax.vmap(lambda own, number: assign_block(jax.random.fold_in(arg_keys[1], 2), own, number, TOK_DEV, EXPERTS, TOP, CAP, 2))(experts_keys, experts_turns).reshape((TOKENS, TOP))
    gates = jnp.clip(jnp.exp(math.log(1.0) - 2.3025851 * jax.random.uniform(arg_keys[2], (TOKENS, TOP), jnp.float32) ** levels(arg_keys[2], (TOKENS, TOP), ((0, 32),), -0.2, 0.2)), 0.1, 1.0)
    expert_inputs = bell_draw(arg_keys[3], (N_REP, EXPERTS, ROWS, D), 1.0, 6.0, ((0, 2), (1, 8)))
    w_in = bell_draw(arg_keys[4], (EXPERTS, D, FF), D ** -0.5, 0.078125, ((0, 8), (2, 2)))
    w_lin = bell_draw(arg_keys[5], (EXPERTS, D, FF), D ** -0.5, 0.078125, ((0, 8), (2, 2)))
    w_out = bell_draw(arg_keys[6], (EXPERTS, FF, D), FF ** -0.5, 0.375, ((0, 8), (1, 2)))
    return {"out_grad": out_grad, "experts": experts, "gates": gates, "expert_inputs": expert_inputs, "w_in": w_in, "w_lin": w_lin, "w_out": w_out}


def slot_table(expert_ids, experts_count, capacity):
    flat = expert_ids.reshape(-1).astype(jnp.int32)
    length = flat.shape[0]
    matches = flat[:, None] == flat[None, :]
    earlier = lax.broadcasted_iota(jnp.int32, (length, length), 1) < lax.broadcasted_iota(jnp.int32, (length, length), 0)
    position = jnp.sum((matches & earlier).astype(jnp.int32), axis=1).astype(jnp.int32)
    target = flat * capacity + position
    slots = lax.broadcasted_iota(jnp.int32, (experts_count * capacity, length), 0)
    return (slots == target[None, :]).astype(jnp.bfloat16)


def rounded(values):
    return lax.optimization_barrier(values.astype(jnp.bfloat16)).astype(jnp.float32)


def reference(out_grad, experts, gates, expert_inputs, w_in, w_lin, w_out):
    blocks = N_REP * N_EXP * N_FFN
    grads = out_grad.reshape(blocks, TOK_DEV, D)
    expert_ids = experts.reshape(blocks, TOK_DEV, TOP)
    gate_vals = gates.reshape(blocks, TOK_DEV, TOP)
    tables = jax.vmap(lambda ids: slot_table(ids, EXPERTS, CAP))(expert_ids)
    weighted = (gate_vals[:, :, :, None] * grads[:, :, None, :].astype(jnp.float32)).reshape(blocks, TOK_DEV * TOP, D).astype(jnp.bfloat16)
    outgoing = jnp.einsum("bsl,bld->bsd", tables.astype(jnp.float32), weighted.astype(jnp.float32)).astype(jnp.bfloat16)
    outgoing = outgoing.reshape(N_REP, N_EXP, N_FFN, EXPERTS, CAP, D)
    routed = jnp.transpose(outgoing, (0, 3, 2, 1, 4, 5)).reshape(N_REP, EXPERTS, ROWS, D)
    gate_w = w_in.astype(jnp.float32)
    linear_w = w_lin.astype(jnp.float32)
    down_w = w_out.astype(jnp.float32)

    def per_replica(carry, items):
        routed_here, inputs_here = items
        routed_f = routed_here.astype(jnp.float32)
        inputs_f = inputs_here.astype(jnp.float32)
        pre_gate = jnp.einsum("erd,edf->erf", inputs_f, gate_w)
        pre_linear = jnp.einsum("erd,edf->erf", inputs_f, linear_w)
        sigmoid_gate = jax.nn.sigmoid(pre_gate)
        activated = pre_gate * sigmoid_gate
        hidden = (activated * pre_linear).astype(jnp.bfloat16).astype(jnp.float32)
        d_hidden = jnp.einsum("erd,efd->erf", routed_f, down_w)
        d_gate = (d_hidden * pre_linear * sigmoid_gate * (1.0 + pre_gate * (1.0 - sigmoid_gate))).astype(jnp.bfloat16).astype(jnp.float32)
        d_linear = (d_hidden * activated).astype(jnp.bfloat16).astype(jnp.float32)
        sum_gate = carry[0] + rounded(jnp.einsum("erd,erf->edf", inputs_f, d_gate))
        sum_linear = carry[1] + rounded(jnp.einsum("erd,erf->edf", inputs_f, d_linear))
        sum_down = carry[2] + rounded(jnp.einsum("erf,erd->efd", hidden, routed_f))
        gate_parts = d_gate.reshape(EXPERTS, ROWS, N_FFN, FF_DEV)
        linear_parts = d_linear.reshape(EXPERTS, ROWS, N_FFN, FF_DEV)
        part_inputs = jnp.einsum("ernf,ednf->enrd", gate_parts, gate_w.reshape(EXPERTS, D, N_FFN, FF_DEV))
        part_inputs = part_inputs + jnp.einsum("ernf,ednf->enrd", linear_parts, linear_w.reshape(EXPERTS, D, N_FFN, FF_DEV))
        slot_grad = jnp.sum(rounded(part_inputs), axis=1).astype(jnp.bfloat16)
        return (sum_gate, sum_linear, sum_down), slot_grad

    start = (jnp.zeros((EXPERTS, D, FF), jnp.float32), jnp.zeros((EXPERTS, D, FF), jnp.float32), jnp.zeros((EXPERTS, FF, D), jnp.float32))
    sums, slot_grads = lax.scan(per_replica, start, (routed, expert_inputs))
    returned = slot_grads.reshape(N_REP, EXPERTS, N_FFN, N_EXP, CAP, D)
    returned = jnp.transpose(returned, (0, 3, 2, 1, 4, 5)).reshape(blocks, EXPERTS * CAP, D)
    combine_table = jnp.sum(tables.astype(jnp.float32).reshape(blocks, EXPERTS * CAP, TOK_DEV, TOP), axis=3)
    grad_input = jnp.einsum("bst,bsd->btd", combine_table, returned.astype(jnp.float32)).astype(jnp.bfloat16)
    return grad_input.reshape(TOKENS, D), sums[0], sums[1], sums[2]
```

```python
import functools

import jax
import jax.numpy as jnp
from jax import lax
from jax.experimental import pallas as pl
from jax.experimental.pallas import tpu as pltpu
from jax.sharding import PartitionSpec as P

LANES = 128
SECTION = 32
F32 = jnp.float32
BF16 = jnp.bfloat16


def nt(left, right):
    return lax.dot_general(left, right, (((1,), (1,)), ((), ())), preferred_element_type=F32)


def tn(left, right):
    return lax.dot_general(left, right, (((0,), (0,)), ((), ())), preferred_element_type=F32)


def local_call(kernel, out_shape, args, flops=0, scratch=(), nbytes=0):
    return pl.pallas_call(
        kernel,
        out_shape=out_shape,
        in_specs=[pl.BlockSpec(memory_space=pltpu.VMEM)] * len(args),
        out_specs=jax.tree.map(lambda _: pl.BlockSpec(memory_space=pltpu.VMEM), out_shape),
        scratch_shapes=list(scratch),
        compiler_params=pltpu.CompilerParams(vmem_limit_bytes=30 * 1024 * 1024),
        cost_estimate=pl.CostEstimate(flops=flops, bytes_accessed=nbytes, transcendentals=0),
    )(*args)


def pack_kernel(capacity, groups, grad_ref, experts_ref, gates_ref, out_ref):
    tokens, width = grad_ref.shape
    experts, gates = experts_ref[...], gates_ref[...]
    lane = lax.broadcasted_iota(jnp.int32, (tokens, LANES), 1)
    expert, section = lane % SECTION, lane // SECTION
    gate = jnp.zeros((tokens, LANES), F32)
    named = jnp.zeros((tokens, LANES), F32)
    for k in range(experts.shape[1]):
        hit = experts[:, k : k + 1] == expert
        gate = gate + jnp.where(hit, gates[:, k : k + 1], 0.0)
        named = named + jnp.where(hit, 1.0, 0.0)
    earlier = jnp.zeros((1, LANES), F32)
    positions = []
    for t in range(tokens):
        positions.append(earlier)
        earlier = earlier + named[t : t + 1]
    block = lax.axis_index("ffn") * groups + lax.axis_index("exp")
    slot = jnp.concatenate(positions, axis=0) + (block * capacity + 1).astype(F32)
    high = gate.astype(BF16).astype(F32)
    middle = (gate - high).astype(BF16).astype(F32)
    low = gate - high - middle
    record = jnp.where(section == 0, high, jnp.where(section == 1, middle, low))
    record = jnp.where(section == 3, jnp.where(named > 0, slot, 0.0), record)
    out_ref[:, :width] = grad_ref[...]
    out_ref[:, width:] = record.astype(BF16)


def pre_kernel(replicas, x_ref, w_in_ref, w_lin_ref, gate_ref, linear_ref, *send_refs):
    share = x_ref.shape[1] // replicas
    me = lax.axis_index("rep")
    for j, send_ref in enumerate(send_refs):
        start = pl.multiple_of((me ^ (j + 1)) * share, LANES)
        send_ref[...] = x_ref[:, pl.ds(start, share)]
    gate_ref[...] = jnp.dot(x_ref[...], w_in_ref[...], preferred_element_type=F32)
    linear_ref[...] = jnp.dot(x_ref[...], w_lin_ref[...], preferred_element_type=F32)


def factor_kernel(replicas, count, *refs):
    pieces, refs = refs[:count], refs[count:]
    gate_ref, linear_ref, w_out_ref = refs[:3]
    d_gate_ref, d_linear_ref, factor_ref, own_ref = refs[3:7]
    send_refs = refs[7 : 7 + replicas - 1]
    t_ref = refs[-1]
    rows = pieces[0].shape[0]
    tokens = rows * count
    width = w_out_ref.shape[1]
    slots = gate_ref.shape[0]
    together = 16 // rows if 16 % rows == 0 and tokens % 16 == 0 else count
    for first in range(0, count, together):
        group = pieces[first : first + together]
        for begin in range(0, width + LANES, 896):
            cols = slice(begin, min(begin + 896, width + LANES))
            block = jnp.concatenate([p[:, cols].astype(F32) for p in group], axis=0)
            t_ref[first * rows : (first + together) * rows, cols] = block.astype(BF16)
    record = t_ref[:, width:].astype(F32)
    lane = lax.broadcasted_iota(jnp.int32, (tokens, LANES), 1)
    expert = lax.axis_index("exp")
    mine = (lane % SECTION == expert) & (lane < 3 * SECTION)
    gates = jnp.sum(jnp.where(mine, record, 0.0), axis=1, keepdims=True)
    slot = jnp.sum(jnp.where(lane == 3 * SECTION + expert, record, 0.0), axis=1, keepdims=True)
    place = lax.broadcasted_iota(jnp.int32, (tokens, slots), 1) + 1
    table = jnp.where(place == slot.astype(jnp.int32), 1.0, 0.0)

    def to_tokens(values):
        return jnp.dot(table, values, preferred_element_type=F32, precision=lax.Precision.HIGHEST)

    pre_gate = to_tokens(gate_ref[...])
    pre_linear = to_tokens(linear_ref[...])
    sigmoid = jax.nn.sigmoid(pre_gate)
    activated = pre_gate * sigmoid
    d_hidden = nt(t_ref[:, :width], w_out_ref[...]) * gates
    d_gate = (d_hidden * pre_linear * sigmoid * (1.0 + pre_gate * (1.0 - sigmoid))).astype(BF16)
    d_linear = (d_hidden * activated).astype(BF16)
    d_gate_ref[...] = d_gate
    d_linear_ref[...] = d_linear
    table = table.astype(BF16)
    factor_ref[:slots] = tn(table, d_gate).astype(BF16)
    factor_ref[slots : 2 * slots] = tn(table, d_linear).astype(BF16)
    factor_ref[2 * slots :] = (activated * pre_linear * gates).astype(BF16)
    share = width // replicas
    me = lax.axis_index("rep")
    own_ref[...] = t_ref[:, pl.ds(pl.multiple_of(me * share, LANES), share)]
    for j, send_ref in enumerate(send_refs):
        send_ref[...] = t_ref[:, pl.ds(pl.multiple_of((me ^ (j + 1)) * share, LANES), share)]


def rows_kernel(d_gate_ref, d_linear_ref, w_in_ref, w_lin_ref, keep_ref, send_ref):
    half, width = keep_ref.shape
    step = 1536 if width % 1536 == 0 else width
    for begin in range(0, width, step):
        cols = slice(begin, begin + step)
        rows = nt(d_gate_ref[...], w_in_ref[cols, :]) + nt(d_linear_ref[...], w_lin_ref[cols, :])
        keep_ref[:, cols] = rows[:half]
        send_ref[:, cols] = rows[half:].astype(BF16)


def sum_kernel(arrived, kept_ref, *refs):
    arrived_refs, keep_ref, send_refs = refs[:arrived], refs[arrived], refs[arrived + 1 :]
    rows, width = keep_ref.shape
    for begin in range(0, width, 1024):
        cols = slice(begin, min(begin + 1024, width))
        total = kept_ref[:, cols]
        for ref in arrived_refs:
            total = total + ref[:, cols].astype(F32)
        keep_ref[:, cols] = total[:rows].astype(keep_ref.dtype)
        for i, ref in enumerate(send_refs):
            ref[:, cols] = total[(i + 1) * rows : (i + 2) * rows].astype(BF16)


def weights_kernel(replicas, slots, *refs):
    x_ref, own_ref, factor_ref = refs[:3]
    others = replicas - 1
    x_others, t_others, f_others = (refs[3 + i * others : 3 + (i + 1) * others] for i in range(3))
    w1_ref, v1_ref, w2_ref = refs[3 + 3 * others :]
    share = own_ref.shape[1]
    me = lax.axis_index("rep")
    factors = (factor_ref, *f_others)
    hidden = jnp.concatenate([f[2 * slots :] for f in factors], axis=0)
    d_gate = jnp.concatenate([f[:slots] for f in factors], axis=0)
    d_linear = jnp.concatenate([f[slots : 2 * slots] for f in factors], axis=0)
    step = 768 if share % 768 == 0 else share
    for begin in range(0, share, step):
        cols = slice(begin, begin + step)
        mine = x_ref[:, pl.ds(pl.multiple_of(me * share + begin, LANES), step)]
        inputs = jnp.concatenate([mine, *(x[:, cols] for x in x_others)], axis=0)
        tokens = jnp.concatenate([own_ref[:, cols], *(t[:, cols] for t in t_others)], axis=0)
        w1_ref[cols, :] = tn(inputs, d_gate)
        v1_ref[cols, :] = tn(inputs, d_linear)
        w2_ref[:, cols] = tn(hidden, tokens)


def swap(values, axis, distance):
    size = lax.axis_size(axis)
    return lax.ppermute(values, axis, [(i, i ^ distance) for i in range(size)])


def body(out_grad, experts, gates, expert_inputs, w_in, w_lin, w_out):
    tokens_here, width = out_grad.shape
    groups, column_groups, replicas = (lax.axis_size(a) for a in ("exp", "ffn", "rep"))
    slots = expert_inputs.shape[2]
    capacity = slots // (column_groups * groups)
    hidden_count = w_in.shape[2]
    share = width // replicas
    tokens = groups * column_groups * tokens_here
    shape = jax.ShapeDtypeStruct
    inputs, gate_w, linear_w, down_w = expert_inputs[0, 0], w_in[0], w_lin[0], w_out[0]
    weight_flops = 2 * tokens * width * hidden_count

    own = local_call(
        functools.partial(pack_kernel, capacity, groups),
        shape((tokens_here, width + LANES), BF16),
        (out_grad, experts, gates),
    )
    column = [own] + [swap(own, "exp", k) for k in range(2, groups, 2)]
    plane = list(column)
    for j in range(1, column_groups):
        plane += [swap(piece, "ffn", j) for piece in column]
    pieces = plane + [swap(piece, "exp", 1) for piece in plane]

    pre_gate, pre_linear, *x_sends = local_call(
        functools.partial(pre_kernel, replicas),
        [shape((slots, hidden_count), F32)] * 2 + [shape((slots, share), BF16)] * (replicas - 1),
        (inputs, gate_w, linear_w),
        flops=2 * weight_flops,
    )
    x_others = [swap(x, "rep", j + 1) for j, x in enumerate(x_sends)]

    d_gate, d_linear, factors, t_own, *t_sends = local_call(
        functools.partial(factor_kernel, replicas, len(pieces)),
        [shape((tokens, hidden_count), BF16)] * 2
        + [shape((2 * slots + tokens, hidden_count), BF16)]
        + [shape((tokens, share), BF16)] * replicas,
        (*pieces, pre_gate, pre_linear, down_w),
        flops=weight_flops,
        scratch=[pltpu.VMEM((tokens, width + LANES), BF16)],
    )
    keep, send = local_call(
        rows_kernel,
        [shape((tokens // 2, width), F32), shape((tokens // 2, width), BF16)],
        (d_gate, d_linear, gate_w, linear_w),
        flops=2 * weight_flops,
    )
    back = swap(send, "exp", 1)
    f_others = [swap(factors, "rep", j) for j in range(1, replicas)]
    t_others = [swap(t, "rep", j + 1) for j, t in enumerate(t_sends)]

    rows = tokens // 2 // column_groups
    keep, *sends = local_call(
        functools.partial(sum_kernel, 1),
        [shape((rows, width), F32)] + [shape((rows, width), BF16)] * (column_groups - 1),
        (keep, back),
    )
    backs = [swap(s, "ffn", j + 1) for j, s in enumerate(sends)]
    keep, *sends = local_call(
        functools.partial(sum_kernel, len(backs)),
        [shape((tokens_here, width), F32)] + [shape((tokens_here, width), BF16)] * (groups // 2 - 1),
        (keep, *backs),
    )
    backs = [swap(s, "exp", 2 * (j + 1)) for j, s in enumerate(sends)]
    grad_w1, grad_v1, grad_w2 = local_call(
        functools.partial(weights_kernel, replicas, slots),
        [shape((share, hidden_count), F32)] * 2 + [shape((hidden_count, share), F32)],
        (inputs, t_own, factors, *x_others, *t_others, *f_others),
        flops=3 * weight_flops,
    )
    (grad_input,) = local_call(
        functools.partial(sum_kernel, len(backs)),
        [shape((tokens_here, width), BF16)],
        (keep, *backs),
    )
    return grad_input, grad_w1[None], grad_v1[None], grad_w2[None]


def solution(mesh):
    in_specs = (
        P(("rep", "exp", "ffn"), None),
        P(("rep", "exp", "ffn"), None),
        P(("rep", "exp", "ffn"), None),
        P("rep", "exp", None, None),
        P("exp", None, "ffn"),
        P("exp", None, "ffn"),
        P("exp", "ffn", None),
    )
    out_specs = (
        P(("rep", "exp", "ffn"), None),
        P("exp", "rep", "ffn"),
        P("exp", "rep", "ffn"),
        P("exp", "ffn", "rep"),
    )
    return jax.shard_map(body, mesh=mesh, in_specs=in_specs, out_specs=out_specs, check_vma=False)
```

```python
import functools

import jax
import jax.numpy as jnp
from jax import lax
from jax.experimental import pallas as pl
from jax.experimental.pallas import tpu as pltpu
from jax.sharding import PartitionSpec as P

LANES = 128
SECTION = 32
F32 = jnp.float32
BF16 = jnp.bfloat16


def nt(left, right):
    return lax.dot_general(left, right, (((1,), (1,)), ((), ())), preferred_element_type=F32)


def tn(left, right):
    return lax.dot_general(left, right, (((0,), (0,)), ((), ())), preferred_element_type=F32)


def local_call(kernel, out_shape, args, flops=0, scratch=(), nbytes=0):
    whole = pl.BlockSpec(memory_space=pltpu.VMEM)
    return pl.pallas_call(
        kernel,
        out_shape=out_shape,
        in_specs=[whole] * len(args),
        out_specs=jax.tree.map(lambda _: whole, out_shape),
        scratch_shapes=list(scratch),
        compiler_params=pltpu.CompilerParams(vmem_limit_bytes=20 * 1024 * 1024),
        cost_estimate=pl.CostEstimate(flops=flops, bytes_accessed=nbytes, transcendentals=0),
    )(*args)


def pack_kernel(capacity, groups, grad_ref, experts_ref, gates_ref, out_ref):
    tokens, width = grad_ref.shape
    experts, gates = experts_ref[...], gates_ref[...]
    lane = lax.broadcasted_iota(jnp.int32, (tokens, LANES), 1)
    expert, section = lane % SECTION, lane // SECTION
    gate = jnp.zeros((tokens, LANES), F32)
    named = jnp.zeros((tokens, LANES), F32)
    for k in range(experts.shape[1]):
        hit = experts[:, k : k + 1] == expert
        gate = gate + jnp.where(hit, gates[:, k : k + 1], 0.0)
        named = named + jnp.where(hit, 1.0, 0.0)
    earlier = jnp.zeros((1, LANES), F32)
    positions = []
    for t in range(tokens):
        positions.append(earlier)
        earlier = earlier + named[t : t + 1]
    block = lax.axis_index("ffn") * groups + lax.axis_index("exp")
    slot = jnp.concatenate(positions, axis=0) + (block * capacity + 1).astype(F32)
    high = gate.astype(BF16).astype(F32)
    middle = (gate - high).astype(BF16).astype(F32)
    low = gate - high - middle
    record = jnp.where(section == 0, high, jnp.where(section == 1, middle, low))
    record = jnp.where(section == 3, jnp.where(named > 0, slot, 0.0), record)
    out_ref[:, :width] = grad_ref[...]
    out_ref[:, width:] = record.astype(BF16)


def stack_kernel(*refs):
    for i, piece in enumerate(refs[:-1]):
        refs[-1][i] = piece[...]


def join_kernel(count, *refs):
    pieces, out_ref = refs[:count], refs[-1]
    width = out_ref.shape[1]
    for begin in range(0, width, 896):
        cols = slice(begin, min(begin + 896, width))
        rows = []
        for ref in pieces:
            parts = [ref[:, cols]] if len(ref.shape) == 2 else [ref[i, :, cols] for i in range(ref.shape[0])]
            rows += [part.astype(F32) for part in parts]
        out_ref[:, cols] = jnp.concatenate(rows, axis=0).astype(BF16)


def share_kernel(x_ref, after_ref, *send_refs):
    del after_ref
    share = send_refs[0].shape[1]
    me = lax.axis_index("rep")
    for i, send_ref in enumerate(send_refs):
        send_ref[...] = x_ref[:, pl.ds(pl.multiple_of((me ^ (i + 1)) * share, LANES), share)]


def pre_kernel(x_ref, w_in_ref, w_lin_ref, after_ref, gate_ref, linear_ref):
    del after_ref
    gate_ref[...] = jnp.dot(x_ref[...], w_in_ref[...], preferred_element_type=F32)
    linear_ref[...] = jnp.dot(x_ref[...], w_lin_ref[...], preferred_element_type=F32)


def main_kernel(replicas, count, *refs):
    pieces, refs = refs[:count], refs[count:]
    gate_ref, linear_ref, w_out_ref, w_in_ref, w_lin_ref = refs[:5]
    keep_ref, back_ref, factor_ref, own_ref, *send_refs, t_ref = refs[5:]
    rows = pieces[0].shape[0]
    tokens = rows * count
    width = w_out_ref.shape[1]
    slots = gate_ref.shape[0]
    for i, piece in enumerate(pieces):
        t_ref[i * rows : (i + 1) * rows, :] = piece[...]
    record = t_ref[:, width:].astype(F32)
    lane = lax.broadcasted_iota(jnp.int32, (tokens, LANES), 1)
    expert = lax.axis_index("exp")
    mine = (lane % SECTION == expert) & (lane < 3 * SECTION)
    gates = jnp.sum(jnp.where(mine, record, 0.0), axis=1, keepdims=True)
    slot = jnp.sum(jnp.where(lane == 3 * SECTION + expert, record, 0.0), axis=1, keepdims=True)
    place = lax.broadcasted_iota(jnp.int32, (tokens, slots), 1) + 1
    table = jnp.where(place == slot.astype(jnp.int32), 1.0, 0.0)

    def to_tokens(values):
        return jnp.dot(table, values, preferred_element_type=F32, precision=lax.Precision.HIGHEST)

    pre_gate = to_tokens(gate_ref[...])
    pre_linear = to_tokens(linear_ref[...])
    sigmoid = jax.nn.sigmoid(pre_gate)
    activated = pre_gate * sigmoid
    d_hidden = nt(t_ref[:, :width], w_out_ref[...]) * gates
    d_gate = (d_hidden * pre_linear * sigmoid * (1.0 + pre_gate * (1.0 - sigmoid))).astype(BF16)
    d_linear = (d_hidden * activated).astype(BF16)
    half = tokens // 2
    step = 1536 if width % 1536 == 0 else width
    for begin in range(0, width, step):
        cols = slice(begin, begin + step)
        out = nt(d_gate, w_in_ref[cols, :]) + nt(d_linear, w_lin_ref[cols, :])
        keep_ref[:, cols] = out[:half]
        back_ref[:, cols] = out[half:].astype(BF16)
    table = table.astype(BF16)
    factor_ref[:slots] = tn(table, d_gate).astype(BF16)
    factor_ref[slots : 2 * slots] = tn(table, d_linear).astype(BF16)
    factor_ref[2 * slots :] = (activated * pre_linear * gates).astype(BF16)
    share = width // replicas
    me = lax.axis_index("rep")
    own_ref[...] = t_ref[:, pl.ds(pl.multiple_of(me * share, LANES), share)]
    for j, send_ref in enumerate(send_refs):
        send_ref[...] = t_ref[:, pl.ds(pl.multiple_of((me ^ (j + 1)) * share, LANES), share)]


def sum_kernel(arrived, cuts, *refs):
    kept_ref, arrived_refs, out_refs = refs[0], refs[1 : 1 + arrived], refs[1 + arrived :]
    width = kept_ref.shape[1]
    for begin in range(0, width, 1024):
        cols = slice(begin, min(begin + 1024, width))
        total = kept_ref[:, cols]
        for ref in arrived_refs:
            total = total + ref[:, cols].astype(F32)
        for ref, (first, last) in zip(out_refs, cuts):
            ref[:, cols] = total[first:last].astype(ref.dtype)


def summed(kept, arrived, cuts, kinds):
    width = kept.shape[1]
    return local_call(
        functools.partial(sum_kernel, len(arrived), cuts),
        [jax.ShapeDtypeStruct((last - first, width), kind) for (first, last), kind in zip(cuts, kinds)],
        (kept, *arrived),
    )


def weights_kernel(replicas, slots, *refs):
    x_ref, own_ref, factor_ref = refs[:3]
    others = replicas - 1
    x_others, t_others, f_others = (refs[3 + i * others : 3 + (i + 1) * others] for i in range(3))
    w1_ref, v1_ref, w2_ref = refs[3 + 3 * others :]
    share = own_ref.shape[1]
    me = lax.axis_index("rep")
    factors = (factor_ref, *f_others)
    hidden = jnp.concatenate([f[2 * slots :] for f in factors], axis=0)
    d_gate = jnp.concatenate([f[:slots] for f in factors], axis=0)
    d_linear = jnp.concatenate([f[slots : 2 * slots] for f in factors], axis=0)
    step = 768 if share % 768 == 0 else share
    for begin in range(0, share, step):
        cols = slice(begin, begin + step)
        mine = x_ref[:, pl.ds(pl.multiple_of(me * share + begin, LANES), step)]
        inputs = jnp.concatenate([mine, *(x[:, cols] for x in x_others)], axis=0)
        tokens = jnp.concatenate([own_ref[:, cols], *(t[:, cols] for t in t_others)], axis=0)
        w1_ref[cols, :] = tn(inputs, d_gate)
        v1_ref[cols, :] = tn(inputs, d_linear)
        w2_ref[:, cols] = tn(hidden, tokens)


def swap(values, axis, distance):
    size = lax.axis_size(axis)
    return lax.ppermute(values, axis, [(i, i ^ distance) for i in range(size)])


def body(out_grad, experts, gates, expert_inputs, w_in, w_lin, w_out):
    tokens_here, width = out_grad.shape
    groups, column_groups, replicas = (lax.axis_size(a) for a in ("exp", "ffn", "rep"))
    slots = expert_inputs.shape[2]
    capacity = slots // (column_groups * groups)
    hidden_count = w_in.shape[2]
    share = width // replicas
    tokens = groups * column_groups * tokens_here
    shape = jax.ShapeDtypeStruct
    inputs, gate_w, linear_w, down_w = expert_inputs[0, 0], w_in[0], w_lin[0], w_out[0]
    weight_flops = 2 * tokens * width * hidden_count

    own = local_call(
        functools.partial(pack_kernel, capacity, groups),
        shape((tokens_here, width + LANES), BF16),
        (out_grad, experts, gates),
        flops=100 * weight_flops,
    )
    across = range(1, column_groups)
    far = [swap(own, "exp", k) for k in range(groups - 2, 0, -2)][::-1]
    beside = [swap(own, "ffn", j) for j in across]
    stack = local_call(stack_kernel, shape((len(far), *own.shape), BF16), tuple(far), flops=50 * weight_flops)
    pieces = [own, stack]
    for j, piece in zip(across, beside):
        pieces += [piece, swap(stack, "ffn", j)]
    x_sends = local_call(
        share_kernel, [shape((slots, share), BF16)] * (replicas - 1), (inputs, far[0])
    )
    x_others = [swap(x, "rep", i + 1) for i, x in enumerate(x_sends)]
    near_rows = local_call(
        functools.partial(join_kernel, len(pieces)),
        shape((tokens // 2, width + LANES), BF16),
        (*pieces, *x_others),
    )
    parts = (near_rows, swap(near_rows, "exp", 1))

    pre_gate, pre_linear = local_call(
        pre_kernel,
        [shape((slots, hidden_count), F32)] * 2,
        (inputs, gate_w, linear_w, far[0]),
        flops=2 * weight_flops,
    )
    keep, send, factors, t_own, *t_sends = local_call(
        functools.partial(main_kernel, replicas, len(parts)),
        [shape((tokens // 2, width), F32), shape((tokens // 2, width), BF16)]
        + [shape((2 * slots + tokens, hidden_count), BF16), shape((tokens, share), BF16)]
        + [shape((tokens, share), BF16)] * (replicas - 1),
        (*parts, pre_gate, pre_linear, down_w, gate_w, linear_w),
        flops=3 * weight_flops,
        scratch=[pltpu.VMEM((tokens, width + LANES), BF16)],
    )
    back = swap(send, "exp", 1)
    t_others = [swap(t, "rep", j + 1) for j, t in enumerate(t_sends)]
    f_others = [swap(factors, "rep", j) for j in range(1, replicas)]

    rows = tokens // 2 // column_groups
    half = rows // 2
    cuts = [(j * rows + h * half, j * rows + (h + 1) * half) for h in (0, 1) for j in range(column_groups)]
    kinds = ([F32] + [BF16] * (column_groups - 1)) * 2
    near, *sends = summed(keep, [back], cuts, kinds)
    near_sends, (away, *away_sends) = sends[: column_groups - 1], sends[column_groups - 1 :]
    cuts = [(i, i + tokens_here) for i in range(0, half, tokens_here)]
    away_backs = [swap(s, "ffn", j + 1) for j, s in enumerate(away_sends)]
    near_backs = [swap(s, "ffn", j + 1) for j, s in enumerate(near_sends)]
    away_sends = summed(away, away_backs, cuts, [BF16] * len(cuts))
    keep, *near_sends = summed(near, near_backs, cuts, [F32] + [BF16] * (len(cuts) - 1))
    backs = [swap(s, "exp", 2 * (j + len(cuts))) for j, s in enumerate(away_sends)]
    backs += [swap(s, "exp", 2 * (j + 1)) for j, s in enumerate(near_sends)]
    grad_w1, grad_v1, grad_w2 = local_call(
        functools.partial(weights_kernel, replicas, slots),
        [shape((share, hidden_count), F32)] * 2 + [shape((hidden_count, share), F32)],
        (inputs, t_own, factors, *x_others, *t_others, *f_others),
        flops=3 * weight_flops,
    )
    (grad_input,) = summed(keep, backs, [(0, tokens_here)], [BF16])
    return grad_input, grad_w1[None], grad_v1[None], grad_w2[None]


def solution(mesh):
    in_specs = (
        P(("rep", "exp", "ffn"), None),
        P(("rep", "exp", "ffn"), None),
        P(("rep", "exp", "ffn"), None),
        P("rep", "exp", None, None),
        P("exp", None, "ffn"),
        P("exp", None, "ffn"),
        P("exp", "ffn", None),
    )
    out_specs = (
        P(("rep", "exp", "ffn"), None),
        P("exp", "rep", "ffn"),
        P("exp", "rep", "ffn"),
        P("exp", "ffn", "rep"),
    )
    return jax.shard_map(body, mesh=mesh, in_specs=in_specs, out_specs=out_specs, check_vma=False)
```

```python
import functools

import jax
import jax.numpy as jnp
from jax import lax
from jax.experimental import pallas as pl
from jax.experimental.pallas import tpu as pltpu
from jax.sharding import PartitionSpec as P

LANES = 128
SECTION = 32
F32 = jnp.float32
BF16 = jnp.bfloat16


def nt(left, right):
    return lax.dot_general(left, right, (((1,), (1,)), ((), ())), preferred_element_type=F32)


def tn(left, right):
    return lax.dot_general(left, right, (((0,), (0,)), ((), ())), preferred_element_type=F32)


def local_call(kernel, out_shape, args, flops=0, scratch=(), nbytes=0, left=False):
    whole = pl.BlockSpec(memory_space=pltpu.VMEM)
    out = pl.BlockSpec(memory_space=pl.ANY) if left else whole
    return pl.pallas_call(
        kernel,
        out_shape=out_shape,
        in_specs=[whole] * len(args),
        out_specs=jax.tree.map(lambda _: out, out_shape),
        scratch_shapes=list(scratch),
        compiler_params=pltpu.CompilerParams(vmem_limit_bytes=20 * 1024 * 1024),
        cost_estimate=pl.CostEstimate(flops=flops, bytes_accessed=nbytes, transcendentals=0),
    )(*args)


def lane_kernel(out_ref):
    out_ref[...] = lax.broadcasted_iota(jnp.int32, out_ref.shape, 1)


def pack_kernel(capacity, groups, grad_ref, experts_ref, gates_ref, lane_ref, out_ref):
    tokens, width = grad_ref.shape
    experts, gates = experts_ref[...], gates_ref[...]
    lane = lane_ref[...]
    expert, section = lane % SECTION, lane // SECTION
    gate = jnp.zeros((tokens, LANES), F32)
    named = jnp.zeros((tokens, LANES), F32)
    for k in range(experts.shape[1]):
        hit = experts[:, k : k + 1] == expert
        gate = gate + jnp.where(hit, gates[:, k : k + 1], 0.0)
        named = named + jnp.where(hit, 1.0, 0.0)
    earlier = jnp.zeros((1, LANES), F32)
    positions = []
    for t in range(tokens):
        positions.append(earlier)
        earlier = earlier + named[t : t + 1]
    block = lax.axis_index("ffn") * groups + lax.axis_index("exp")
    slot = jnp.concatenate(positions, axis=0) + (block * capacity + 1).astype(F32)
    high = gate.astype(BF16).astype(F32)
    middle = (gate - high).astype(BF16).astype(F32)
    low = gate - high - middle
    record = jnp.where(section == 0, high, jnp.where(section == 1, middle, low))
    record = jnp.where(section == 3, jnp.where(named > 0, slot, 0.0), record)
    out_ref[:, :width] = grad_ref[...]
    out_ref[:, width:] = record.astype(BF16)


def stack_kernel(*refs):
    for i, piece in enumerate(refs[:-1]):
        refs[-1][i] = piece[...]


def join_kernel(order, *refs):
    out_ref = refs[-1]
    width = out_ref.shape[1]
    for begin in range(0, width, 896):
        cols = slice(begin, min(begin + 896, width))
        rows = [refs[stack][place, :, cols].astype(F32) for stack, place in order]
        out_ref[:, cols] = jnp.concatenate(rows, axis=0).astype(BF16)


def share_kernel(x_ref, after_ref, *send_refs):
    del after_ref
    share = send_refs[0].shape[1]
    me = lax.axis_index("rep")
    for i, send_ref in enumerate(send_refs):
        send_ref[...] = x_ref[:, pl.ds(pl.multiple_of((me ^ (i + 1)) * share, LANES), share)]


def pre_kernel(x_ref, w_in_ref, w_lin_ref, *refs):
    gate_ref, linear_ref, both_ref = refs[-3:]
    hidden_count = w_in_ref.shape[1]
    gate_ref[...] = jnp.dot(x_ref[...], w_in_ref[...], preferred_element_type=F32)
    linear_ref[...] = jnp.dot(x_ref[...], w_lin_ref[...], preferred_element_type=F32)
    both_ref[:hidden_count] = w_in_ref[...].T
    both_ref[hidden_count:] = w_lin_ref[...].T


def main_kernel(replicas, near_ref, away_ref, gate_ref, linear_ref, w_out_ref, both_ref, *refs):
    keep_ref, back_ref, factor_ref, *send_refs = refs
    half = near_ref.shape[0]
    tokens = 2 * half
    width = w_out_ref.shape[1]
    slots = gate_ref.shape[0]
    record = jnp.concatenate([near_ref[:, width:], away_ref[:, width:]], axis=0).astype(F32)
    lane = lax.broadcasted_iota(jnp.int32, (tokens, LANES), 1)
    expert = lax.axis_index("exp")
    mine = (lane % SECTION == expert) & (lane < 3 * SECTION)
    gates = jnp.sum(jnp.where(mine, record, 0.0), axis=1, keepdims=True)
    slot = jnp.sum(jnp.where(lane == 3 * SECTION + expert, record, 0.0), axis=1, keepdims=True)
    place = lax.broadcasted_iota(jnp.int32, (tokens, slots), 1) + 1
    table = jnp.where(place == slot.astype(jnp.int32), 1.0, 0.0)

    def to_tokens(values):
        return jnp.dot(table, values, preferred_element_type=F32, precision=lax.Precision.HIGHEST)

    pre_gate = to_tokens(gate_ref[...])
    pre_linear = to_tokens(linear_ref[...])
    sigmoid = jax.nn.sigmoid(pre_gate)
    activated = pre_gate * sigmoid
    rows = jnp.concatenate([near_ref[:, :width], away_ref[:, :width]], axis=0)
    d_hidden = (nt(w_out_ref[...], rows) * jnp.broadcast_to(gates, (tokens, w_out_ref.shape[0])).T).T
    d_gate = (d_hidden * pre_linear * sigmoid * (1.0 + pre_gate * (1.0 - sigmoid))).astype(BF16)
    d_linear = (d_hidden * activated).astype(BF16)
    d_both = jnp.concatenate([d_gate, d_linear], axis=1)
    step = 1536 if width % 1536 == 0 else width
    for begin in range(0, width, step):
        cols = slice(begin, begin + step)
        out = jnp.dot(d_both, both_ref[:, cols], preferred_element_type=F32)
        keep_ref[:, cols] = out[:half]
        back_ref[:, cols] = out[half:].astype(BF16)
    table = table.astype(BF16)
    factor_ref[:slots] = tn(table, d_gate).astype(BF16)
    factor_ref[slots : 2 * slots] = tn(table, d_linear).astype(BF16)
    factor_ref[2 * slots :] = (activated * pre_linear * gates).astype(BF16)
    share = width // replicas
    me = lax.axis_index("rep")
    for j, send_ref in enumerate(send_refs):
        columns = pl.ds(pl.multiple_of((me ^ (j + 1)) * share, LANES), share)
        send_ref[:half] = near_ref[:, columns]
        send_ref[half:] = away_ref[:, columns]


def sum_kernel(arrived, cuts, *refs):
    kept_ref, arrived_refs, out_refs = refs[0], refs[1 : 1 + arrived], refs[1 + arrived :]
    width = kept_ref.shape[1]
    for begin in range(0, width, 1024):
        cols = slice(begin, min(begin + 1024, width))
        total = kept_ref[:, cols]
        for ref in arrived_refs:
            total = total + ref[:, cols].astype(F32)
        for ref, (first, last) in zip(out_refs, cuts):
            ref[:, cols] = total[first:last].astype(ref.dtype)


def summed(kept, arrived, cuts, kinds):
    width = kept.shape[1]
    return local_call(
        functools.partial(sum_kernel, len(arrived), cuts),
        [jax.ShapeDtypeStruct((last - first, width), kind) for (first, last), kind in zip(cuts, kinds)],
        (kept, *arrived),
    )


def weights_kernel(replicas, slots, x_ref, near_ref, away_ref, factor_ref, *refs):
    others = replicas - 1
    x_others, t_others, f_others = (refs[i * others : (i + 1) * others] for i in range(3))
    outs, held, sem = refs[3 * others : 3 * others + 3], refs[-4:-1], refs[-1]
    share = outs[0].shape[0]
    start = lax.axis_index("rep") * share
    factors = (factor_ref, *f_others)
    hidden = jnp.concatenate([f[2 * slots :] for f in factors], axis=0)
    d_gate = jnp.concatenate([f[:slots] for f in factors], axis=0)
    d_linear = jnp.concatenate([f[slots : 2 * slots] for f in factors], axis=0)
    step = 768 if share % 768 == 0 else share
    copies = []
    for begin in range(0, share, step):
        cols = slice(begin, begin + step)
        columns = pl.ds(pl.multiple_of(start + begin, LANES), step)
        inputs = jnp.concatenate([x_ref[:, columns], *(x[:, cols] for x in x_others)], axis=0)
        held[0][cols, :] = tn(inputs, d_gate)
        held[1][cols, :] = tn(inputs, d_linear)
        tokens = jnp.concatenate(
            [near_ref[:, columns], away_ref[:, columns], *(t[:, cols] for t in t_others)], axis=0
        )
        held[2][:, cols] = tn(hidden, tokens)
        for i, at in enumerate(((cols, slice(None)), (cols, slice(None)), (slice(None), cols))):
            copies.append(pltpu.make_async_copy(held[i].at[at], outs[i].at[at], sem.at[len(copies)]))
            copies[-1].start()
    for copy in copies:
        copy.wait()


def swap(values, axis, distance):
    size = lax.axis_size(axis)
    return lax.ppermute(values, axis, [(i, i ^ distance) for i in range(size)])


def body(out_grad, experts, gates, expert_inputs, w_in, w_lin, w_out):
    tokens_here, width = out_grad.shape
    groups, column_groups, replicas = (lax.axis_size(a) for a in ("exp", "ffn", "rep"))
    slots = expert_inputs.shape[2]
    capacity = slots // (column_groups * groups)
    hidden_count = w_in.shape[2]
    share = width // replicas
    tokens = groups * column_groups * tokens_here
    shape = jax.ShapeDtypeStruct
    inputs, gate_w, linear_w, down_w = expert_inputs[0, 0], w_in[0], w_lin[0], w_out[0]
    weight_flops = 2 * tokens * width * hidden_count

    lanes = local_call(lane_kernel, shape((tokens_here, LANES), jnp.int32), (), flops=100 * weight_flops)
    own = local_call(
        functools.partial(pack_kernel, capacity, groups),
        shape((tokens_here, width + LANES), BF16),
        (out_grad, experts, gates, lanes),
        flops=100 * weight_flops,
    )
    across = range(1, column_groups)
    steps = range(0, groups, 2)
    column = [own] + [swap(own, "exp", k) for k in steps[:0:-1]][::-1]
    half = len(column) // 2
    stacks = [
        local_call(stack_kernel, shape((half, *own.shape), BF16), tuple(part), flops=50 * weight_flops)
        for part in (column[:half], column[half:])
    ]
    pieces = list(stacks)
    for j in across:
        pieces += [swap(stack, "ffn", j) for stack in stacks]
    steps = [0, groups - 2, *range(2, groups - 2, 2)]
    order = [(2 * j + k // 2 // half, k // 2 % half) for j in range(column_groups) for k in steps]
    x_sends = local_call(
        share_kernel, [shape((slots, share), BF16)] * (replicas - 1), (inputs, own)
    )
    x_others = [swap(x, "rep", i + 1) for i, x in enumerate(x_sends)]
    pre_gate, pre_linear, both = local_call(
        pre_kernel,
        [shape((slots, hidden_count), F32)] * 2 + [shape((2 * hidden_count, width), BF16)],
        (inputs, gate_w, linear_w, stacks[0]),
        flops=2 * weight_flops,
    )
    near_rows = local_call(
        functools.partial(join_kernel, order),
        shape((tokens // 2, width + LANES), BF16),
        (*pieces, *x_others, pre_gate),
    )
    parts = (near_rows, swap(near_rows, "exp", 1))

    keep, send, factors, *t_sends = local_call(
        functools.partial(main_kernel, replicas),
        [shape((tokens // 2, width), F32), shape((tokens // 2, width), BF16)]
        + [shape((2 * slots + tokens, hidden_count), BF16)]
        + [shape((tokens, share), BF16)] * (replicas - 1),
        (*parts, pre_gate, pre_linear, down_w, both),
        flops=3 * weight_flops,
    )
    back = swap(send, "exp", 1)
    t_others = [swap(t, "rep", j + 1) for j, t in enumerate(t_sends)]
    f_others = [swap(factors, "rep", j) for j in range(1, replicas)]

    rows = tokens // 2 // column_groups
    half = rows // 2
    cuts = [(j * rows + h * half, j * rows + (h + 1) * half) for h in (0, 1) for j in range(column_groups)]
    kinds = ([F32] + [BF16] * (column_groups - 1)) * 2
    near, *sends = summed(keep, [back], cuts, kinds)
    near_sends, (away, *away_sends) = sends[: column_groups - 1], sends[column_groups - 1 :]
    cuts = [(i, i + tokens_here) for i in range(0, half, tokens_here)]
    away_backs = [swap(s, "ffn", j + 1) for j, s in enumerate(away_sends)]
    near_backs = [swap(s, "ffn", j + 1) for j, s in enumerate(near_sends)]
    away_sends = summed(away, away_backs, cuts, [BF16] * len(cuts))
    keep, *near_sends = summed(near, near_backs, cuts, [F32] + [BF16] * (len(cuts) - 1))
    backs = [swap(s, "exp", k) for k, s in zip(steps[len(cuts) :], away_sends)]
    backs += [swap(s, "exp", k) for k, s in zip(steps[1:], near_sends)]
    grads = [(share, hidden_count)] * 2 + [(hidden_count, share)]
    grad_w1, grad_v1, grad_w2 = local_call(
        functools.partial(weights_kernel, replicas, slots),
        [shape(grad, F32) for grad in grads],
        (inputs, *parts, factors, *x_others, *t_others, *f_others),
        flops=3 * weight_flops,
        scratch=[pltpu.VMEM(grad, F32) for grad in grads] + [pltpu.SemaphoreType.DMA((12,))],
        left=True,
    )
    (grad_input,) = summed(keep, backs, [(0, tokens_here)], [BF16])
    return grad_input, grad_w1[None], grad_v1[None], grad_w2[None]


def solution(mesh):
    in_specs = (
        P(("rep", "exp", "ffn"), None),
        P(("rep", "exp", "ffn"), None),
        P(("rep", "exp", "ffn"), None),
        P("rep", "exp", None, None),
        P("exp", None, "ffn"),
        P("exp", None, "ffn"),
        P("exp", "ffn", None),
    )
    out_specs = (
        P(("rep", "exp", "ffn"), None),
        P("exp", "rep", "ffn"),
        P("exp", "rep", "ffn"),
        P("exp", "ffn", "rep"),
    )
    return jax.shard_map(body, mesh=mesh, in_specs=in_specs, out_specs=out_specs, check_vma=False)
```

```python
import functools

import jax
import jax.numpy as jnp
from jax import lax
from jax.experimental import pallas as pl
from jax.experimental.pallas import tpu as pltpu
from jax.sharding import PartitionSpec as P

LANES = 128
SECTION = 32
F32 = jnp.float32
BF16 = jnp.bfloat16


def nt(left, right):
    return lax.dot_general(left, right, (((1,), (1,)), ((), ())), preferred_element_type=F32)


def tn(left, right):
    return lax.dot_general(left, right, (((0,), (0,)), ((), ())), preferred_element_type=F32)


def local_call(kernel, out_shape, args, flops=0, scratch=(), nbytes=0, left=False):
    whole = pl.BlockSpec(memory_space=pltpu.VMEM)
    out = pl.BlockSpec(memory_space=pl.ANY) if left else whole
    return pl.pallas_call(
        kernel,
        out_shape=out_shape,
        in_specs=[whole] * len(args),
        out_specs=jax.tree.map(lambda _: out, out_shape),
        scratch_shapes=list(scratch),
        compiler_params=pltpu.CompilerParams(vmem_limit_bytes=20 * 1024 * 1024),
        cost_estimate=pl.CostEstimate(flops=flops, bytes_accessed=nbytes, transcendentals=0),
    )(*args)


def lane_kernel(out_ref):
    out_ref[...] = lax.broadcasted_iota(jnp.int32, out_ref.shape, 1)


def pack_kernel(capacity, groups, grad_ref, experts_ref, gates_ref, lane_ref, out_ref):
    tokens, width = grad_ref.shape
    experts, gates = experts_ref[...], gates_ref[...]
    lane = lane_ref[...]
    expert, section = lane % SECTION, lane // SECTION
    gate = jnp.zeros((tokens, LANES), F32)
    named = jnp.zeros((tokens, LANES), F32)
    for k in range(experts.shape[1]):
        hit = experts[:, k : k + 1] == expert
        gate = gate + jnp.where(hit, gates[:, k : k + 1], 0.0)
        named = named + jnp.where(hit, 1.0, 0.0)
    earlier = jnp.zeros((1, LANES), F32)
    positions = []
    for t in range(tokens):
        positions.append(earlier)
        earlier = earlier + named[t : t + 1]
    block = lax.axis_index("ffn") * groups + lax.axis_index("exp")
    slot = jnp.concatenate(positions, axis=0) + (block * capacity + 1).astype(F32)
    high = gate.astype(BF16).astype(F32)
    middle = (gate - high).astype(BF16).astype(F32)
    low = gate - high - middle
    record = jnp.where(section == 0, high, jnp.where(section == 1, middle, low))
    record = jnp.where(section == 3, jnp.where(named > 0, slot, 0.0), record)
    out_ref[:, :width] = grad_ref[...]
    out_ref[:, width:] = record.astype(BF16)


def stack_kernel(*refs):
    for i, piece in enumerate(refs[:-1]):
        refs[-1][i] = piece[...]


def join_kernel(order, *refs):
    out_ref = refs[-1]
    width = out_ref.shape[1]
    for begin in range(0, width, 896):
        cols = slice(begin, min(begin + 896, width))
        rows = [refs[stack][place, :, cols].astype(F32) for stack, place in order]
        out_ref[:, cols] = jnp.concatenate(rows, axis=0).astype(BF16)


def share_kernel(x_ref, after_ref, *send_refs):
    del after_ref
    share = send_refs[0].shape[1]
    me = lax.axis_index("rep")
    for i, send_ref in enumerate(send_refs):
        send_ref[...] = x_ref[:, pl.ds(pl.multiple_of((me ^ (i + 1)) * share, LANES), share)]


def pre_kernel(x_ref, w_in_ref, w_lin_ref, *refs):
    parts_ref, both_ref = refs[-2:]
    hidden_count = w_in_ref.shape[1]
    for i, weight_ref in enumerate((w_in_ref, w_lin_ref)):
        rest = jnp.dot(x_ref[...], weight_ref[...], preferred_element_type=F32)
        for part in range(3):
            rounded = rest.astype(BF16)
            parts_ref[:, (2 * part + i) * hidden_count : (2 * part + i + 1) * hidden_count] = rounded
            rest = rest - rounded.astype(F32)
    both_ref[:hidden_count] = w_in_ref[...].T
    both_ref[hidden_count:] = w_lin_ref[...].T


def main_kernel(replicas, near_ref, away_ref, parts_ref, w_out_ref, both_ref, *refs):
    keep_ref, back_ref, factor_ref, *send_refs = refs
    half = near_ref.shape[0]
    tokens = 2 * half
    width = w_out_ref.shape[1]
    slots = parts_ref.shape[0]
    record = jnp.concatenate([near_ref[:, width:], away_ref[:, width:]], axis=0).astype(F32)
    lane = lax.broadcasted_iota(jnp.int32, (tokens, LANES), 1)
    expert = lax.axis_index("exp")
    mine = (lane % SECTION == expert) & (lane < 3 * SECTION)
    gates = jnp.sum(jnp.where(mine, record, 0.0), axis=1, keepdims=True)
    slot = jnp.sum(jnp.where(lane == 3 * SECTION + expert, record, 0.0), axis=1, keepdims=True)
    place = lax.broadcasted_iota(jnp.int32, (tokens, slots), 1) + 1
    table = jnp.where(place == slot.astype(jnp.int32), 1.0, 0.0).astype(BF16)
    parts = jnp.dot(table, parts_ref[...], preferred_element_type=F32)
    hidden_count = w_out_ref.shape[0]
    pre_gate, pre_linear = (
        sum(parts[:, i * hidden_count : (i + 1) * hidden_count] for i in range(first, 6, 2)) for first in (0, 1)
    )
    sigmoid = jax.nn.sigmoid(pre_gate)
    activated = pre_gate * sigmoid
    rows = jnp.concatenate([near_ref[:, :width], away_ref[:, :width]], axis=0)
    d_hidden = (nt(w_out_ref[...], rows) * jnp.broadcast_to(gates, (tokens, w_out_ref.shape[0])).T).T
    d_gate = (d_hidden * pre_linear * sigmoid * (1.0 + pre_gate * (1.0 - sigmoid))).astype(BF16)
    d_linear = (d_hidden * activated).astype(BF16)
    d_both = jnp.concatenate([d_gate, d_linear], axis=1)
    step = 1536 if width % 1536 == 0 else width
    for begin in range(0, width, step):
        cols = slice(begin, begin + step)
        out = jnp.dot(d_both, both_ref[:, cols], preferred_element_type=F32)
        keep_ref[:, cols] = out[:half]
        back_ref[:, cols] = out[half:].astype(BF16)
    factor_ref[:slots] = tn(table, d_gate).astype(BF16)
    factor_ref[slots : 2 * slots] = tn(table, d_linear).astype(BF16)
    factor_ref[2 * slots :] = (activated * pre_linear * gates).astype(BF16)
    share = width // replicas
    me = lax.axis_index("rep")
    for j, send_ref in enumerate(send_refs):
        columns = pl.ds(pl.multiple_of((me ^ (j + 1)) * share, LANES), share)
        send_ref[:half] = near_ref[:, columns]
        send_ref[half:] = away_ref[:, columns]


def sum_kernel(arrived, cuts, *refs):
    kept_ref, arrived_refs, out_refs = refs[0], refs[1 : 1 + arrived], refs[1 + arrived :]
    width = kept_ref.shape[1]
    for begin in range(0, width, 1024):
        cols = slice(begin, min(begin + 1024, width))
        total = kept_ref[:, cols]
        for ref in arrived_refs:
            total = total + ref[:, cols].astype(F32)
        for ref, (first, last) in zip(out_refs, cuts):
            ref[:, cols] = total[first:last].astype(ref.dtype)


def summed(kept, arrived, cuts, kinds):
    width = kept.shape[1]
    return local_call(
        functools.partial(sum_kernel, len(arrived), cuts),
        [jax.ShapeDtypeStruct((last - first, width), kind) for (first, last), kind in zip(cuts, kinds)],
        (kept, *arrived),
    )


def weights_kernel(replicas, slots, x_ref, near_ref, away_ref, factor_ref, *refs):
    others = replicas - 1
    x_others, t_others, f_others = (refs[i * others : (i + 1) * others] for i in range(3))
    outs, held, sem = refs[3 * others : 3 * others + 3], refs[-4:-1], refs[-1]
    share = outs[0].shape[0]
    start = lax.axis_index("rep") * share
    factors = (factor_ref, *f_others)
    hidden = jnp.concatenate([f[2 * slots :] for f in factors], axis=0)
    d_gate = jnp.concatenate([f[:slots] for f in factors], axis=0)
    d_linear = jnp.concatenate([f[slots : 2 * slots] for f in factors], axis=0)
    step = 768 if share % 768 == 0 else share
    copies = []
    for begin in range(0, share, step):
        cols = slice(begin, begin + step)
        columns = pl.ds(pl.multiple_of(start + begin, LANES), step)
        inputs = jnp.concatenate([x_ref[:, columns], *(x[:, cols] for x in x_others)], axis=0)
        held[0][cols, :] = tn(inputs, d_gate)
        held[1][cols, :] = tn(inputs, d_linear)
        tokens = jnp.concatenate(
            [near_ref[:, columns], away_ref[:, columns], *(t[:, cols] for t in t_others)], axis=0
        )
        held[2][:, cols] = tn(hidden, tokens)
        for i, at in enumerate(((cols, slice(None)), (cols, slice(None)), (slice(None), cols))):
            copies.append(pltpu.make_async_copy(held[i].at[at], outs[i].at[at], sem.at[len(copies)]))
            copies[-1].start()
    for copy in copies:
        copy.wait()


def swap(values, axis, distance):
    size = lax.axis_size(axis)
    return lax.ppermute(values, axis, [(i, i ^ distance) for i in range(size)])


def body(out_grad, experts, gates, expert_inputs, w_in, w_lin, w_out):
    tokens_here, width = out_grad.shape
    groups, column_groups, replicas = (lax.axis_size(a) for a in ("exp", "ffn", "rep"))
    slots = expert_inputs.shape[2]
    capacity = slots // (column_groups * groups)
    hidden_count = w_in.shape[2]
    share = width // replicas
    tokens = groups * column_groups * tokens_here
    shape = jax.ShapeDtypeStruct
    inputs, gate_w, linear_w, down_w = expert_inputs[0, 0], w_in[0], w_lin[0], w_out[0]
    weight_flops = 2 * tokens * width * hidden_count

    lanes = local_call(lane_kernel, shape((tokens_here, LANES), jnp.int32), (), flops=100 * weight_flops)
    own = local_call(
        functools.partial(pack_kernel, capacity, groups),
        shape((tokens_here, width + LANES), BF16),
        (out_grad, experts, gates, lanes),
        flops=100 * weight_flops,
    )
    across = range(1, column_groups)
    steps = range(0, groups, 2)
    column = [own] + [swap(own, "exp", k) for k in steps[:0:-1]][::-1]
    half = len(column) // 2
    stacks = [
        local_call(stack_kernel, shape((half, *own.shape), BF16), tuple(part), flops=50 * weight_flops)
        for part in (column[:half], column[half:])
    ]
    pieces = list(stacks)
    for j in across:
        pieces += [swap(stack, "ffn", j) for stack in stacks]
    steps = [0, groups - 2, *range(2, groups - 2, 2)]
    order = [(2 * j + k // 2 // half, k // 2 % half) for j in range(column_groups) for k in steps]
    x_sends = local_call(
        share_kernel, [shape((slots, share), BF16)] * (replicas - 1), (inputs, own)
    )
    x_others = [swap(x, "rep", i + 1) for i, x in enumerate(x_sends)]
    split, both = local_call(
        pre_kernel,
        [shape((slots, 6 * hidden_count), BF16), shape((2 * hidden_count, width), BF16)],
        (inputs, gate_w, linear_w, stacks[0]),
        flops=2 * weight_flops,
    )
    near_rows = local_call(
        functools.partial(join_kernel, order),
        shape((tokens // 2, width + LANES), BF16),
        (*pieces, *x_others, split),
    )
    parts = (near_rows, swap(near_rows, "exp", 1))

    keep, send, factors, *t_sends = local_call(
        functools.partial(main_kernel, replicas),
        [shape((tokens // 2, width), F32), shape((tokens // 2, width), BF16)]
        + [shape((2 * slots + tokens, hidden_count), BF16)]
        + [shape((tokens, share), BF16)] * (replicas - 1),
        (*parts, split, down_w, both),
        flops=3 * weight_flops,
    )
    back = swap(send, "exp", 1)
    t_others = [swap(t, "rep", j + 1) for j, t in enumerate(t_sends)]
    f_others = [swap(factors, "rep", j) for j in range(1, replicas)]

    rows = tokens // 2 // column_groups
    half = rows // 2
    cuts = [(j * rows + h * half, j * rows + (h + 1) * half) for h in (0, 1) for j in range(column_groups)]
    kinds = ([F32] + [BF16] * (column_groups - 1)) * 2
    near, *sends = summed(keep, [back], cuts, kinds)
    near_sends, (away, *away_sends) = sends[: column_groups - 1], sends[column_groups - 1 :]
    cuts = [(i, i + tokens_here) for i in range(0, half, tokens_here)]
    away_backs = [swap(s, "ffn", j + 1) for j, s in enumerate(away_sends)]
    near_backs = [swap(s, "ffn", j + 1) for j, s in enumerate(near_sends)]
    away_sends = summed(away, away_backs, cuts, [BF16] * len(cuts))
    keep, *near_sends = summed(near, near_backs, cuts, [F32] + [BF16] * (len(cuts) - 1))
    backs = [swap(s, "exp", k) for k, s in zip(steps[len(cuts) :], away_sends)]
    backs += [swap(s, "exp", k) for k, s in zip(steps[1:], near_sends)]
    grads = [(share, hidden_count)] * 2 + [(hidden_count, share)]
    grad_w1, grad_v1, grad_w2 = local_call(
        functools.partial(weights_kernel, replicas, slots),
        [shape(grad, F32) for grad in grads],
        (inputs, *parts, factors, *x_others, *t_others, *f_others),
        flops=3 * weight_flops,
        scratch=[pltpu.VMEM(grad, F32) for grad in grads] + [pltpu.SemaphoreType.DMA((12,))],
        left=True,
    )
    (grad_input,) = summed(keep, backs, [(0, tokens_here)], [BF16])
    return grad_input, grad_w1[None], grad_v1[None], grad_w2[None]


def solution(mesh):
    in_specs = (
        P(("rep", "exp", "ffn"), None),
        P(("rep", "exp", "ffn"), None),
        P(("rep", "exp", "ffn"), None),
        P("rep", "exp", None, None),
        P("exp", None, "ffn"),
        P("exp", None, "ffn"),
        P("exp", "ffn", None),
    )
    out_specs = (
        P(("rep", "exp", "ffn"), None),
        P("exp", "rep", "ffn"),
        P("exp", "rep", "ffn"),
        P("exp", "ffn", "rep"),
    )
    return jax.shard_map(body, mesh=mesh, in_specs=in_specs, out_specs=out_specs, check_vma=False)
```

```python
import functools

import jax
import jax.numpy as jnp
from jax import lax
from jax.experimental import pallas as pl
from jax.experimental.pallas import tpu as pltpu
from jax.sharding import PartitionSpec as P

LANES = 128
SECTION = 32
F32 = jnp.float32
BF16 = jnp.bfloat16


def nt(left, right):
    return lax.dot_general(left, right, (((1,), (1,)), ((), ())), preferred_element_type=F32)


def tn(left, right):
    return lax.dot_general(left, right, (((0,), (0,)), ((), ())), preferred_element_type=F32)


def local_call(kernel, out_shape, args, flops=0, scratch=(), nbytes=0, left=False):
    whole = pl.BlockSpec(memory_space=pltpu.VMEM)
    out = pl.BlockSpec(memory_space=pl.ANY) if left else whole
    return pl.pallas_call(
        kernel,
        out_shape=out_shape,
        in_specs=[whole] * len(args),
        out_specs=jax.tree.map(lambda _: out, out_shape),
        scratch_shapes=list(scratch),
        compiler_params=pltpu.CompilerParams(vmem_limit_bytes=20 * 1024 * 1024),
        cost_estimate=pl.CostEstimate(flops=flops, bytes_accessed=nbytes, transcendentals=0),
    )(*args)


def lane_kernel(out_ref):
    out_ref[...] = lax.broadcasted_iota(jnp.int32, out_ref.shape, 1)


def pack_kernel(capacity, groups, grad_ref, experts_ref, gates_ref, lane_ref, out_ref):
    tokens, width = grad_ref.shape
    experts, gates = experts_ref[...], gates_ref[...]
    lane = lane_ref[...]
    expert, section = lane % SECTION, lane // SECTION
    gate = jnp.zeros((tokens, LANES), F32)
    named = jnp.zeros((tokens, LANES), F32)
    for k in range(experts.shape[1]):
        hit = experts[:, k : k + 1] == expert
        gate = gate + jnp.where(hit, gates[:, k : k + 1], 0.0)
        named = named + jnp.where(hit, 1.0, 0.0)
    earlier = jnp.zeros((1, LANES), F32)
    positions = []
    for t in range(tokens):
        positions.append(earlier)
        earlier = earlier + named[t : t + 1]
    block = lax.axis_index("ffn") * groups + lax.axis_index("exp")
    slot = jnp.concatenate(positions, axis=0) + (block * capacity + 1).astype(F32)
    high = gate.astype(BF16).astype(F32)
    middle = (gate - high).astype(BF16).astype(F32)
    low = gate - high - middle
    record = jnp.where(section == 0, high, jnp.where(section == 1, middle, low))
    record = jnp.where(section == 3, jnp.where(named > 0, slot, 0.0), record)
    out_ref[:, :width] = grad_ref[...]
    out_ref[:, width:] = record.astype(BF16)


def stack_kernel(*refs):
    for i, piece in enumerate(refs[:-1]):
        refs[-1][i] = piece[...]


def join_kernel(order, *refs):
    out_ref = refs[-1]
    width = out_ref.shape[1]
    for begin in range(0, width, 896):
        cols = slice(begin, min(begin + 896, width))
        rows = [refs[stack][place, :, cols].astype(F32) for stack, place in order]
        out_ref[:, cols] = jnp.concatenate(rows, axis=0).astype(BF16)


def share_kernel(x_ref, after_ref, *send_refs):
    del after_ref
    share = send_refs[0].shape[1]
    me = lax.axis_index("rep")
    for i, send_ref in enumerate(send_refs):
        columns = pl.ds(pl.multiple_of((me ^ (i + 1)) * share, LANES), share)
        send_ref[...] = x_ref[: send_ref.shape[0], columns]


def pre_kernel(x_ref, w_in_ref, w_lin_ref, *refs):
    parts_ref, both_ref = refs[-2:]
    hidden_count = w_in_ref.shape[1]
    for i, weight_ref in enumerate((w_in_ref, w_lin_ref)):
        rest = jnp.dot(x_ref[...], weight_ref[...], preferred_element_type=F32)
        for part in range(3):
            rounded = rest.astype(BF16)
            parts_ref[:, (2 * part + i) * hidden_count : (2 * part + i + 1) * hidden_count] = rounded
            rest = rest - rounded.astype(F32)
    both_ref[:hidden_count] = w_in_ref[...].T
    both_ref[hidden_count:] = w_lin_ref[...].T


def main_kernel(replicas, near_ref, away_ref, parts_ref, w_out_ref, both_ref, x_ref, *refs):
    keep_ref, back_ref, factor_ref, *send_refs = refs
    half = near_ref.shape[0]
    tokens = 2 * half
    width = w_out_ref.shape[1]
    slots = parts_ref.shape[0]
    record = jnp.concatenate([near_ref[:, width:], away_ref[:, width:]], axis=0).astype(F32)
    lane = lax.broadcasted_iota(jnp.int32, (tokens, LANES), 1)
    expert = lax.axis_index("exp")
    mine = (lane % SECTION == expert) & (lane < 3 * SECTION)
    gates = jnp.sum(jnp.where(mine, record, 0.0), axis=1, keepdims=True)
    slot = jnp.sum(jnp.where(lane == 3 * SECTION + expert, record, 0.0), axis=1, keepdims=True)
    place = lax.broadcasted_iota(jnp.int32, (tokens, slots), 1) + 1
    table = jnp.where(place == slot.astype(jnp.int32), 1.0, 0.0).astype(BF16)
    parts = jnp.dot(table, parts_ref[...], preferred_element_type=F32)
    hidden_count = w_out_ref.shape[0]
    pre_gate, pre_linear = (
        sum(parts[:, i * hidden_count : (i + 1) * hidden_count] for i in range(first, 6, 2)) for first in (0, 1)
    )
    sigmoid = jax.nn.sigmoid(pre_gate)
    activated = pre_gate * sigmoid
    rows = jnp.concatenate([near_ref[:, :width], away_ref[:, :width]], axis=0)
    d_hidden = (nt(w_out_ref[...], rows) * jnp.broadcast_to(gates, (tokens, w_out_ref.shape[0])).T).T
    d_gate = (d_hidden * pre_linear * sigmoid * (1.0 + pre_gate * (1.0 - sigmoid))).astype(BF16)
    d_linear = (d_hidden * activated).astype(BF16)
    d_both = jnp.concatenate([d_gate, d_linear], axis=1)
    step = 1536 if width % 1536 == 0 else width
    for begin in range(0, width, step):
        cols = slice(begin, begin + step)
        out = jnp.dot(d_both, both_ref[:, cols], preferred_element_type=F32)
        keep_ref[:, cols] = out[:half]
        back_ref[:, cols] = out[half:].astype(BF16)
    factor_ref[:slots] = tn(table, d_gate).astype(BF16)
    factor_ref[slots : 2 * slots] = tn(table, d_linear).astype(BF16)
    factor_ref[2 * slots :] = (activated * pre_linear * gates).astype(BF16)
    share = width // replicas
    me = lax.axis_index("rep")
    for j, send_ref in enumerate(send_refs):
        columns = pl.ds(pl.multiple_of((me ^ (j + 1)) * share, LANES), share)
        send_ref[:half] = near_ref[:, columns]
        send_ref[half:tokens] = away_ref[:, columns]
        send_ref[tokens:] = x_ref[slots - (send_ref.shape[0] - tokens) :, columns]


def sum_kernel(arrived, cuts, *refs):
    kept_ref, arrived_refs, out_refs = refs[0], refs[1 : 1 + arrived], refs[1 + arrived :]
    width = kept_ref.shape[1]
    for begin in range(0, width, 1024):
        cols = slice(begin, min(begin + 1024, width))
        total = kept_ref[:, cols]
        for ref in arrived_refs:
            total = total + ref[:, cols].astype(F32)
        for ref, (first, last) in zip(out_refs, cuts):
            ref[:, cols] = total[first:last].astype(ref.dtype)


def summed(kept, arrived, cuts, kinds):
    width = kept.shape[1]
    return local_call(
        functools.partial(sum_kernel, len(arrived), cuts),
        [jax.ShapeDtypeStruct((last - first, width), kind) for (first, last), kind in zip(cuts, kinds)],
        (kept, *arrived),
    )


def weights_kernel(replicas, slots, x_ref, near_ref, away_ref, factor_ref, *refs):
    others = replicas - 1
    x_others, t_others, f_others = (refs[i * others : (i + 1) * others] for i in range(3))
    outs, held, sem = refs[3 * others : 3 * others + 3], refs[-4:-1], refs[-1]
    share = outs[0].shape[0]
    count = 2 * near_ref.shape[0]
    start = lax.axis_index("rep") * share
    factors = (factor_ref, *f_others)
    hidden = jnp.concatenate([f[2 * slots :] for f in factors], axis=0)
    d_gate = jnp.concatenate([f[:slots] for f in factors], axis=0)
    d_linear = jnp.concatenate([f[slots : 2 * slots] for f in factors], axis=0)
    step = 768 if share % 768 == 0 else share
    copies = []
    for begin in range(0, share, step):
        cols = slice(begin, begin + step)
        columns = pl.ds(pl.multiple_of(start + begin, LANES), step)
        inputs = jnp.concatenate([x_ref[:, columns], *(x[:, cols] for pair in zip(x_others, (t.at[count:] for t in t_others)) for x in pair)], axis=0)
        held[0][cols, :] = tn(inputs, d_gate)
        held[1][cols, :] = tn(inputs, d_linear)
        tokens = jnp.concatenate(
            [near_ref[:, columns], away_ref[:, columns], *(t[:count, cols] for t in t_others)], axis=0
        )
        held[2][:, cols] = tn(hidden, tokens)
        for i, at in enumerate(((cols, slice(None)), (cols, slice(None)), (slice(None), cols))):
            copies.append(pltpu.make_async_copy(held[i].at[at], outs[i].at[at], sem.at[len(copies)]))
            copies[-1].start()
    for copy in copies:
        copy.wait()


def swap(values, axis, distance):
    size = lax.axis_size(axis)
    return lax.ppermute(values, axis, [(i, i ^ distance) for i in range(size)])


def body(out_grad, experts, gates, expert_inputs, w_in, w_lin, w_out):
    tokens_here, width = out_grad.shape
    groups, column_groups, replicas = (lax.axis_size(a) for a in ("exp", "ffn", "rep"))
    slots = expert_inputs.shape[2]
    capacity = slots // (column_groups * groups)
    hidden_count = w_in.shape[2]
    share = width // replicas
    tokens = groups * column_groups * tokens_here
    shape = jax.ShapeDtypeStruct
    inputs, gate_w, linear_w, down_w = expert_inputs[0, 0], w_in[0], w_lin[0], w_out[0]
    weight_flops = 2 * tokens * width * hidden_count

    lanes = local_call(lane_kernel, shape((tokens_here, LANES), jnp.int32), (), flops=100 * weight_flops)
    own = local_call(
        functools.partial(pack_kernel, capacity, groups),
        shape((tokens_here, width + LANES), BF16),
        (out_grad, experts, gates, lanes),
        flops=100 * weight_flops,
    )
    across = range(1, column_groups)
    early = slots // 64 * 56
    steps = range(0, groups, 2)
    taken = [0, groups - 2, *range(2, groups - 2, 2)]
    column = [own] + [swap(own, "exp", k) for k in taken[1:]]
    half = len(column) // 2
    stacks = [
        local_call(stack_kernel, shape((half, *own.shape), BF16), tuple(part), flops=50 * weight_flops)
        for part in (column[:half], column[half:])
    ]
    pieces = list(stacks)
    for j in across:
        pieces += [swap(stack, "ffn", j) for stack in stacks]
    steps = [0, groups - 2, *range(2, groups - 2, 2)]
    order = [(2 * j + taken.index(k) // half, taken.index(k) % half) for j in range(column_groups) for k in steps]
    x_sends = local_call(
        share_kernel, [shape((early, share), BF16)] * (replicas - 1), (inputs, own)
    )
    x_others = [swap(x, "rep", i + 1) for i, x in enumerate(x_sends)]
    split, both = local_call(
        pre_kernel,
        [shape((slots, 6 * hidden_count), BF16), shape((2 * hidden_count, width), BF16)],
        (inputs, gate_w, linear_w, stacks[0]),
        flops=2 * weight_flops,
    )
    near_rows = local_call(
        functools.partial(join_kernel, order),
        shape((tokens // 2, width + LANES), BF16),
        (*pieces, *x_others, split),
    )
    parts = (near_rows, swap(near_rows, "exp", 1))

    keep, send, factors, *t_sends = local_call(
        functools.partial(main_kernel, replicas),
        [shape((tokens // 2, width), F32), shape((tokens // 2, width), BF16)]
        + [shape((2 * slots + tokens, hidden_count), BF16)]
        + [shape((tokens + slots - early, share), BF16)] * (replicas - 1),
        (*parts, split, down_w, both, inputs),
        flops=3 * weight_flops,
    )
    back = swap(send, "exp", 1)
    t_others = [swap(t, "rep", j + 1) for j, t in enumerate(t_sends)]
    f_others = [swap(factors, "rep", j) for j in range(1, replicas)]

    rows = tokens // 2 // column_groups
    half = rows // 2
    cuts = [(j * rows + h * half, j * rows + (h + 1) * half) for h in (0, 1) for j in range(column_groups)]
    kinds = ([F32] + [BF16] * (column_groups - 1)) * 2
    near, *sends = summed(keep, [back], cuts, kinds)
    near_sends, (away, *away_sends) = sends[: column_groups - 1], sends[column_groups - 1 :]
    cuts = [(i, i + tokens_here) for i in range(0, half, tokens_here)]
    away_backs = [swap(s, "ffn", j + 1) for j, s in enumerate(away_sends)]
    near_backs = [swap(s, "ffn", j + 1) for j, s in enumerate(near_sends)]
    away_sends = summed(away, away_backs, cuts, [BF16] * len(cuts))
    keep, *near_sends = summed(near, near_backs, cuts, [F32] + [BF16] * (len(cuts) - 1))
    backs = [swap(s, "exp", k) for k, s in zip(steps[len(cuts) :], away_sends)]
    backs += [swap(s, "exp", k) for k, s in zip(steps[1:], near_sends)]
    grads = [(share, hidden_count)] * 2 + [(hidden_count, share)]
    grad_w1, grad_v1, grad_w2 = local_call(
        functools.partial(weights_kernel, replicas, slots),
        [shape(grad, F32) for grad in grads],
        (inputs, *parts, factors, *x_others, *t_others, *f_others),
        flops=3 * weight_flops,
        scratch=[pltpu.VMEM(grad, F32) for grad in grads] + [pltpu.SemaphoreType.DMA((12,))],
        left=True,
    )
    (grad_input,) = summed(keep, backs, [(0, tokens_here)], [BF16])
    return grad_input, grad_w1[None], grad_v1[None], grad_w2[None]


def solution(mesh):
    in_specs = (
        P(("rep", "exp", "ffn"), None),
        P(("rep", "exp", "ffn"), None),
        P(("rep", "exp", "ffn"), None),
        P("rep", "exp", None, None),
        P("exp", None, "ffn"),
        P("exp", None, "ffn"),
        P("exp", "ffn", None),
    )
    out_specs = (
        P(("rep", "exp", "ffn"), None),
        P("exp", "rep", "ffn"),
        P("exp", "rep", "ffn"),
        P("exp", "ffn", "rep"),
    )
    return jax.shard_map(body, mesh=mesh, in_specs=in_specs, out_specs=out_specs, check_vma=False)
```
